32 devices in a mesh: sect: 4 (over y, x), blk: 8 (over z, core).
Axes of the slice: x: 2, y: 2, z: 4, core: 2. Of those that a mesh axis runs over, the one named last changes fastest.
Arguments:
- theta: bfloat16 [4, 4096, 2048], P('sect', 'blk'), may hold values from -6 to 6
- left_env: bfloat16 [4, 8, 4096, 4096], P('sect', None, 'blk'), may hold values from -0.125 to 0.125
- sector_ids: int32 [4, 4096], P('sect'), may hold values from 0 to 15, never falling along the last dimension, each value on 1 to 2560 neighbouring positions
- local_ops: float32 [4, 8, 16, 16], P('sect'), may hold values from -0.5 to 0.5
- edge_env: float32 [128, 128], replicated, may hold values from -0.5 to 0.5
Outputs:
- updated: bfloat16 [4, 4096, 2048], P('sect', 'blk')
- outgoing: float32 [4, 128, 128], P('sect')
The draws below stay inside these ranges and needn't reach their ends.
Inputs may be any that keep to these rules, and one draw needn't show every extreme that they name: `sector_ids`: within each section the sector numbers never fall along the rows; each sector holds 1 to 2560 rows and one holds exactly 2560.
All inputs are finite; a program needn't handle non-finite values.
Results may differ from the reference program's by a relative error of at most 0.00165.
Values may be sent and summed in bfloat16 or wider, within the bound.
A program may use at most 128 MiB of HBM per device.

```python
import math
import jax
import jax.numpy as jnp
import numpy as np
from jax import lax

D = 4096
W = 8
P2 = 16
NSEC = 16
CW = 128
MOST = 2560
N_SECT = 4


def steps_of(stream_key, dims, shards, smallest, top_value):
    loudness, own = 1.0, jax.random.fold_in(stream_key, 6)
    for position, blocks in shards:
        steps = jnp.exp(jax.random.uniform(jax.random.fold_in(own, position), (blocks,), jnp.float32, smallest / len(shards), top_value / len(shards)))
        loudness = loudness * jnp.repeat(steps, dims[position] // blocks).reshape([-1 if axis == position else 1 for axis in range(len(dims))])
    return loudness


def length_profile(number_of, total, limit, slope):
    weights = [(1 << 20) // math.isqrt(rank ** slope) + 1 for rank in range(2, number_of + 1)]
    surplus, holding = total - limit - (number_of - 1), [1] * (number_of - 1)
    while surplus > 0:
        candidates = [i for i in range(number_of - 1) if holding[i] < limit]
        pool, left = sum([weights[i] for i in candidates]), surplus
        for i in candidates:
            extra = min(limit - holding[i], max(1, left * weights[i] // pool), surplus)
            holding[i] = holding[i] + extra
            surplus = surplus - extra
    return np.array([limit] + holding)


def ragged(own_key, number_of, total, reach, lean):
    if number_of == 2:
        one = jax.random.randint(own_key, (), max(1, total - reach), min(reach, total - 1) + 1)
        return jnp.stack([one, total - one])
    sizes = jnp.asarray(length_profile(number_of, total, reach, lean), jnp.int32)
    couples = (number_of - 1) // 2
    giver, taker = sizes[1:1 + 2 * couples:2], sizes[2:2 + 2 * couples:2]
    margin = jnp.minimum(giver - 1, reach - taker)
    passed = jax.random.randint(jax.random.fold_in(own_key, 1), (couples,), 0, 1 << 20) % (margin + 1)
    sizes = sizes.at[1:1 + 2 * couples:2].set(giver - passed).at[2:2 + 2 * couples:2].set(taker + passed)
    return sizes[jax.random.permutation(jax.random.fold_in(own_key, 2), number_of)]


def noise(own_key, shape, deviation, bound, cuts=(), held_as=jnp.bfloat16):
    gain = steps_of(own_key, shape, cuts, -0.22, 0.18) if cuts else 1.0
    drawn = jax.random.normal(own_key, shape, jnp.float32) * deviation * gain
    return jnp.minimum(jnp.maximum(drawn, -bound), bound).astype(held_as)


def setup_inputs(seed: int = 0) -> dict:
    seeds = jax.random.split(jax.random.key(seed), 6)
    theta = noise(seeds[0], (N_SECT, D, P2 * CW), 1.0, 6.0, ((0, 4), (1, 8)))
    left_env = noise(seeds[1], (N_SECT, W, D, D), MOST ** -0.5, 0.125, ((0, 4), (2, 8)))
    sector_ids = jax.vmap(lambda own: jnp.searchsorted(jnp.cumsum(ragged(own, NSEC, D, MOST, 2)), jnp.arange(D), side="right"))(jax.random.split(seeds[2], N_SECT)).reshape((N_SECT, D)).astype(jnp.int32)
    local_ops = noise(seeds[3], (N_SECT, W, P2, P2), (W * P2) ** -0.5, 0.5, ((0, 4),), jnp.float32)
    edge_env = noise(seeds[4], (CW, CW), CW ** -0.5, 0.5, (), jnp.float32)
    return {"theta": theta, "left_env": left_env, "sector_ids": sector_ids, "local_ops": local_ops, "edge_env": edge_env}


def one_section(theta_s, env_s, sec_s, ops_s):
    same = sec_s[:, None] == sec_s[None, :]
    theta_f = theta_s.astype(jnp.float32)

    def apply_one(env_w):
        masked = jnp.where(same, env_w, jnp.zeros_like(env_w)).astype(jnp.float32)
        return jnp.dot(masked, theta_f, precision=lax.Precision.HIGHEST)
    applied = lax.map(apply_one, env_s)
    applied = applied.reshape(W, D, P2, CW)
    acted = jnp.einsum('wpq,wiqc->ipc', ops_s, applied, precision=lax.Precision.HIGHEST)
    intersection = jnp.einsum('ipc,ipd->cd', theta_f.reshape(D, P2, CW), acted, precision=lax.Precision.HIGHEST)
    transfer = intersection * jnp.sqrt(jnp.float32(CW)) / jnp.sqrt(jnp.sum(intersection * intersection) + 1e-06)
    return (acted, transfer)

def reference(theta, left_env, sector_ids, local_ops, edge_env):
    incoming = edge_env
    updated = []
    outgoing = []
    for sect_no in range(N_SECT):
        acted, transfer = one_section(theta[sect_no], left_env[sect_no], sector_ids[sect_no], local_ops[sect_no])
        result = jnp.einsum('ipc,cd->ipd', acted, incoming, precision=lax.Precision.HIGHEST)
        updated.append(result.reshape(D, P2 * CW).astype(jnp.bfloat16))
        leaving = jnp.dot(incoming, transfer, precision=lax.Precision.HIGHEST)
        outgoing.append(leaving)
        incoming = leaving
    return (jnp.stack(updated), jnp.stack(outgoing))
```

```python
import functools
import jax
import jax.numpy as jnp
from jax import lax
from jax.experimental import pallas as pl
from jax.experimental.pallas import tpu as pltpu
from jax.sharding import PartitionSpec as P

MOST = 2560
WIDE = 256
AHEAD = 3
MESH = pl.DeviceIdType.MESH


def split(x):
    hi = x.astype(jnp.bfloat16)
    lo = (x - hi.astype(jnp.float32)).astype(jnp.bfloat16)
    return hi, lo


def kernel(
    dims,
    theta_hbm, env_hbm, my_sec, sec_all, ops, edge,
    out, outgoing,
    env, got, applied, acted, part, rs_buf, xs_buf, all_buf,
    env_sem, own_sem, recv, send, rs_send, rs_recv, xs_send, xs_recv, ag_send, ag_recv,
):
    n_sect, n_blk, rows, depth, width, chain, phys, cols = dims
    chips = n_blk // 2
    steps = width // WIDE
    per = WIDE // cols
    reach = (MOST - 2) // rows + 1
    piece = cols // n_blk
    s = lax.axis_index("sect")
    b = lax.axis_index("blk")
    z, c = b // 2, b % 2
    mate = z * 2 + (1 - c)

    def near(x, y):
        return jnp.abs(x - y) <= reach

    def block(k, at):
        return got.at[k, pl.ds(pl.multiple_of(at * rows, rows), rows), :]

    def env_copy(w):
        return pltpu.make_async_copy(
            env_hbm.at[0, w], env.at[pl.ds(w * rows, rows), :], env_sem.at[w]
        )

    def own_copy(k):
        return pltpu.make_async_copy(
            theta_hbm.at[0, :, pl.ds(pl.multiple_of(k * WIDE, WIDE), WIDE)],
            block(k, b),
            own_sem.at[k],
        )

    def move(k, at, way, target):
        return pltpu.make_async_remote_copy(
            src_ref=block(k, at),
            dst_ref=block(k, at),
            send_sem=send.at[k, at, way],
            recv_sem=recv.at[k, at],
            device_id=(s, target),
            device_id_type=MESH,
        )

    def own_sends(k, act):
        @pl.when(z < chips - 1)
        def _():
            act(move(k, b, 0, b + 2))

        @pl.when(z > 0)
        def _():
            act(move(k, b, 1, b - 2))

        act(move(k, b, 2, mate))

    def passes(k, d, way, first, act):
        src = z - d if way == 0 else z + d
        nxt = z + 1 if way == 0 else z - 1
        at = src * 2 + c
        valid = (src >= 0) & (src < chips) & (near(at, b) | near(at, mate))

        @pl.when(valid)
        def _():
            if first:
                move(k, at, way, mate).wait_recv()

            @pl.when((nxt >= 0) & (nxt < chips) & (near(at, nxt * 2) | near(at, nxt * 2 + 1)))
            def _():
                act(move(k, at, way, nxt * 2 + c))

            @pl.when(near(at, mate))
            def _():
                act(move(k, at, 2, mate))

    def start(copy):
        copy.start()

    def wait_sent(copy):
        copy.wait_send()

    for w in range(chain):
        env_copy(w).start()

    @pl.loop(0, steps)
    def _(k):
        own_copy(k).start()

    barrier = pltpu.get_barrier_semaphore()
    for off in range(1, n_blk):
        pl.semaphore_signal(barrier, inc=1, device_id=(s, lax.rem(b + off, n_blk)), device_id_type=MESH)
    for off in range(1, n_sect):
        pl.semaphore_signal(barrier, inc=1, device_id=(lax.rem(s + off, n_sect), b), device_id_type=MESH)
    pl.semaphore_wait(barrier, n_blk - 1 + n_sect - 1)

    @pl.loop(0, min(AHEAD, steps))
    def _(k):
        own_copy(k).wait()
        own_sends(k, start)

    acted[...] = jnp.zeros_like(acted)
    applied[...] = jnp.zeros_like(applied)

    for w in range(chain):
        env_copy(w).wait()

    @pl.loop(0, rows // 16)
    def _(t):
        at = pl.multiple_of(t * 16, 16)
        keep = (my_sec[pl.ds(at, 16), :] == sec_all[...]).astype(jnp.float32).astype(jnp.bfloat16)
        for w in range(chain):
            here = pl.ds(pl.multiple_of(w * rows + at, 16), 16)
            env[here, :] = env[here, :] * keep

    tile = min(512, chain * rows)

    def multiply(k, at):
        @pl.loop(0, chain * rows // tile)
        def _(m):
            here = pl.ds(pl.multiple_of(m * tile, tile), tile)
            applied[here, :] += jnp.dot(
                env[here, pl.ds(pl.multiple_of(at * rows, rows), rows)],
                got[k, pl.ds(pl.multiple_of(at * rows, rows), rows), :],
                preferred_element_type=jnp.float32,
            )

    def act_on(k):
        @pl.loop(0, rows // 16)
        def _(t):
            at = pl.multiple_of(t * 16, 16)
            here = pl.ds(at, 16)
            terms = []
            for w in range(chain):
                for q in range(per):
                    there = pl.ds(pl.multiple_of(w * rows + at, 16), 16)
                    terms.append((w, q, applied[there, q * cols:(q + 1) * cols]))
                    applied[there, q * cols:(q + 1) * cols] = jnp.zeros((16, cols), jnp.float32)
            for p in range(phys):
                total = acted[here, p * cols:(p + 1) * cols]
                for w, q, x in terms:
                    total += ops[(w * phys + p) * phys + k * per + q] * x
                acted[here, p * cols:(p + 1) * cols] = total

    @pl.loop(0, steps * chips + 1)
    def _(t):
        k, d = t // chips, t % chips

        @pl.when((d == 0) & (k + AHEAD < steps))
        def _():
            own_copy(k + AHEAD).wait()
            own_sends(k + AHEAD, start)

        @pl.when((d > 0) & (k < steps))
        def _():
            passes(k, d, 0, True, start)
            passes(k, d, 1, True, start)

        @pl.when(t > 0)
        def _():
            kk, dd = (t - 1) // chips, (t - 1) % chips

            @pl.loop(0, 4)
            def _(j):
                side, lane = j // 2, j % 2
                src = z - dd + 2 * dd * side
                at = src * 2 + lane
                valid = (src >= 0) & (src < chips) & near(at, b) & ((dd > 0) | (side == 0))

                @pl.when(valid)
                def _():
                    @pl.when(lane != c)
                    def _():
                        move(kk, at, 2, mate).wait_recv()

                    multiply(kk, at)

            @pl.when(dd == chips - 1)
            def _():
                act_on(kk)

    total = jnp.zeros((cols, 2 * cols), jnp.float32)
    for p in range(phys):
        hi, lo = split(acted[:, p * cols:(p + 1) * cols])
        mine = got[p // per, pl.ds(pl.multiple_of(b * rows, rows), rows), (p % per) * cols:(p % per + 1) * cols]
        total += lax.dot_general(
            mine, jnp.concatenate([hi, lo], axis=1), (((0,), (0,)), ((), ())),
            preferred_element_type=jnp.float32,
        )
    total = total[:, :cols] + total[:, cols:]
    for j in range(n_blk):
        part[j] = total[j * piece:(j + 1) * piece]

    def rs_copy(src, dst, off):
        return pltpu.make_async_remote_copy(
            src_ref=part.at[dst], dst_ref=rs_buf.at[src],
            send_sem=rs_send.at[off], recv_sem=rs_recv.at[src],
            device_id=(s, dst), device_id_type=MESH,
        )

    for off in range(1, n_blk):
        rs_copy(b, lax.rem(b + off, n_blk), off).start()
    summed = part[b]
    for off in range(1, n_blk):
        peer = lax.rem(b + off, n_blk)
        rs_copy(peer, peer, off).wait_recv()
        summed += rs_buf[peer]
    xs_buf[s] = summed

    def xs_copy(src, dst, off):
        return pltpu.make_async_remote_copy(
            src_ref=xs_buf.at[src], dst_ref=xs_buf.at[src],
            send_sem=xs_send.at[off], recv_sem=xs_recv.at[src],
            device_id=(dst, b), device_id_type=MESH,
        )

    for off in range(1, n_sect):
        xs_copy(s, lax.rem(s + off, n_sect), off).start()
    for off in range(1, n_sect):
        peer = lax.rem(s + off, n_sect)
        xs_copy(peer, peer, off).wait_recv()

    def ag_copy(src, dst, off):
        return pltpu.make_async_remote_copy(
            src_ref=xs_buf, dst_ref=all_buf.at[src],
            send_sem=ag_send.at[off], recv_sem=ag_recv.at[src],
            device_id=(s, dst), device_id_type=MESH,
        )

    for off in range(1, n_blk):
        ag_copy(b, lax.rem(b + off, n_blk), off).start()
    all_buf[b] = xs_buf[...]
    for off in range(1, n_blk):
        peer = lax.rem(b + off, n_blk)
        ag_copy(peer, peer, off).wait_recv()

    incoming = edge[...]
    leaving = edge[...]
    for sect in range(n_sect):
        inter = jnp.concatenate([all_buf[j, sect] for j in range(n_blk)], axis=0)
        scale = jnp.sqrt(jnp.float32(cols)) / jnp.sqrt(jnp.sum(inter * inter, keepdims=True) + 1e-06)
        incoming = jnp.where(sect <= s, leaving, incoming)
        leaving = jnp.where(
            sect <= s,
            jnp.dot(leaving, inter * scale, precision=lax.Precision.HIGHEST, preferred_element_type=jnp.float32),
            leaving,
        )
    outgoing[0] = leaving

    hi, lo = split(incoming)
    weights = jnp.concatenate(
        [jnp.concatenate([hi, lo], axis=1), jnp.concatenate([hi, jnp.zeros_like(lo)], axis=1)], axis=0
    )
    for p in range(phys):
        hi, lo = split(acted[:, p * cols:(p + 1) * cols])
        res = jnp.dot(jnp.concatenate([hi, lo], axis=1), weights, preferred_element_type=jnp.float32)
        out[0, :, p * cols:(p + 1) * cols] = (res[:, :cols] + res[:, cols:]).astype(jnp.bfloat16)

    for off in range(1, n_blk):
        peer = lax.rem(b + off, n_blk)
        rs_copy(b, peer, off).wait_send()
        ag_copy(b, peer, off).wait_send()
    for off in range(1, n_sect):
        xs_copy(s, lax.rem(s + off, n_sect), off).wait_send()

    @pl.loop(0, steps)
    def _(k):
        own_sends(k, wait_sent)

        @pl.loop(1, chips)
        def _(d):
            passes(k, d, 0, False, wait_sent)
            passes(k, d, 1, False, wait_sent)


def per_device(n_sect, n_blk, theta, left_env, sector_ids, local_ops, edge_env):
    rows, width = theta.shape[1], theta.shape[2]
    chain, depth = left_env.shape[1], left_env.shape[3]
    phys = local_ops.shape[2]
    cols = width // phys
    steps = width // WIDE
    piece = cols // n_blk
    dims = (n_sect, n_blk, rows, depth, width, chain, phys, cols)
    my_sec = lax.dynamic_slice_in_dim(sector_ids[0], lax.axis_index("blk") * rows, rows, 0)[:, None]
    any_spec = pl.BlockSpec(memory_space=pl.ANY)
    vmem = pl.BlockSpec(memory_space=pltpu.VMEM)
    smem = pl.BlockSpec(memory_space=pltpu.SMEM)
    dma = pltpu.SemaphoreType.DMA
    return pl.pallas_call(
        functools.partial(kernel, dims),
        out_shape=(
            jax.ShapeDtypeStruct((1, rows, width), jnp.bfloat16),
            jax.ShapeDtypeStruct((1, cols, cols), jnp.float32),
        ),
        in_specs=[any_spec, any_spec, vmem, vmem, smem, vmem],
        out_specs=(vmem, vmem),
        scratch_shapes=[
            pltpu.VMEM((chain * rows, depth), jnp.bfloat16),
            pltpu.VMEM((steps, depth, WIDE), jnp.bfloat16),
            pltpu.VMEM((chain * rows, WIDE), jnp.float32),
            pltpu.VMEM((rows, width), jnp.float32),
            pltpu.VMEM((n_blk, piece, cols), jnp.float32),
            pltpu.VMEM((n_blk, piece, cols), jnp.float32),
            pltpu.VMEM((n_sect, piece, cols), jnp.float32),
            pltpu.VMEM((n_blk, n_sect, piece, cols), jnp.float32),
            dma((chain,)), dma((steps,)), dma((steps, n_blk)), dma((steps, n_blk, 3)),
            dma((n_blk,)), dma((n_blk,)), dma((n_sect,)), dma((n_sect,)), dma((n_blk,)), dma((n_blk,)),
        ],
        compiler_params=pltpu.CompilerParams(
            collective_id=0, has_side_effects=True, vmem_limit_bytes=62 * 1024 * 1024
        ),
        cost_estimate=pl.CostEstimate(
            flops=2 * chain * rows * depth * width,
            bytes_accessed=2 * chain * rows * depth,
            transcendentals=0,
        ),
    )(theta, left_env, my_sec, sector_ids, local_ops.reshape(-1), edge_env)


def solution(mesh):
    placed = (
        P("sect", "blk", None),
        P("sect", None, "blk", None),
        P("sect", None),
        P("sect", None, None, None),
        P(),
    )
    return jax.shard_map(
        functools.partial(per_device, mesh.shape["sect"], mesh.shape["blk"]),
        mesh=mesh,
        in_specs=placed,
        out_specs=(P("sect", "blk", None), P("sect", None, None)),
        check_vma=False,
    )
```

```python
import functools
import jax
import jax.numpy as jnp
from jax import lax
from jax.experimental import pallas as pl
from jax.experimental.pallas import tpu as pltpu
from jax.sharding import PartitionSpec as P

MOST = 2560
WIDE = 256
AHEAD = 3
MESH = pl.DeviceIdType.MESH


def split(x):
    hi = x.astype(jnp.bfloat16)
    lo = (x - hi.astype(jnp.float32)).astype(jnp.bfloat16)
    return hi, lo


def kernel(
    dims,
    theta_hbm, env_hbm, my_sec, sec_all, mix, edge,
    out, outgoing,
    env, got, applied, acted, part, rs_buf, xs_buf, all_buf,
    env_sem, own_sem, recv, send, rs_send, rs_recv, xs_send, xs_recv, ag_send, ag_recv,
):
    n_sect, n_blk, rows, depth, width, chain, phys, cols = dims
    chips = n_blk // 2
    steps = width // WIDE
    per = WIDE // cols
    reach = (MOST - 2) // rows + 1
    piece = cols // n_blk
    s = lax.axis_index("sect")
    b = lax.axis_index("blk")
    z, c = b // 2, b % 2
    mate = z * 2 + (1 - c)

    def near(x, y):
        return jnp.abs(x - y) <= reach

    def block(k, at):
        return got.at[k, pl.ds(pl.multiple_of(at * rows, rows), rows), :]

    def env_copy(w):
        return pltpu.make_async_copy(
            env_hbm.at[0, w], env.at[pl.ds(w * rows, rows), :], env_sem.at[w]
        )

    def own_copy(k):
        return pltpu.make_async_copy(
            theta_hbm.at[0, :, pl.ds(pl.multiple_of(k * WIDE, WIDE), WIDE)],
            block(k, b),
            own_sem.at[k],
        )

    def move(k, at, way, target):
        return pltpu.make_async_remote_copy(
            src_ref=block(k, at),
            dst_ref=block(k, at),
            send_sem=send.at[k, at, way],
            recv_sem=recv.at[k, at],
            device_id=(s, target),
            device_id_type=MESH,
        )

    def own_sends(k, act):
        @pl.when(z < chips - 1)
        def _():
            act(move(k, b, 0, b + 2))

        @pl.when(z > 0)
        def _():
            act(move(k, b, 1, b - 2))

        act(move(k, b, 2, mate))

    def passes(k, d, way, first, act):
        src = z - d if way == 0 else z + d
        nxt = z + 1 if way == 0 else z - 1
        at = src * 2 + c
        valid = (src >= 0) & (src < chips) & (near(at, b) | near(at, mate))

        @pl.when(valid)
        def _():
            if first:
                move(k, at, way, mate).wait_recv()

            @pl.when((nxt >= 0) & (nxt < chips) & (near(at, nxt * 2) | near(at, nxt * 2 + 1)))
            def _():
                act(move(k, at, way, nxt * 2 + c))

            @pl.when(near(at, mate))
            def _():
                act(move(k, at, 2, mate))

    def start(copy):
        copy.start()

    def wait_sent(copy):
        copy.wait_send()

    for w in range(chain):
        env_copy(w).start()

    @pl.loop(0, steps)
    def _(k):
        own_copy(k).start()

    barrier = pltpu.get_barrier_semaphore()
    for off in range(1, n_blk):
        pl.semaphore_signal(barrier, inc=1, device_id=(s, lax.rem(b + off, n_blk)), device_id_type=MESH)
    for off in range(1, n_sect):
        pl.semaphore_signal(barrier, inc=1, device_id=(lax.rem(s + off, n_sect), b), device_id_type=MESH)
    pl.semaphore_wait(barrier, n_blk - 1 + n_sect - 1)

    @pl.loop(0, min(AHEAD, steps))
    def _(k):
        own_copy(k).wait()
        own_sends(k, start)

    acted[...] = jnp.zeros_like(acted)
    applied[...] = jnp.zeros_like(applied)

    for w in range(chain):
        env_copy(w).wait()

    @pl.loop(0, rows // 16)
    def _(t):
        at = pl.multiple_of(t * 16, 16)
        keep = (my_sec[pl.ds(at, 16), :] == sec_all[...]).astype(jnp.float32).astype(jnp.bfloat16)
        for w in range(chain):
            here = pl.ds(pl.multiple_of(w * rows + at, 16), 16)
            env[here, :] = env[here, :] * keep

    tile = min(512, chain * rows)

    def multiply(k, at):
        @pl.loop(0, chain * rows // tile)
        def _(m):
            here = pl.ds(pl.multiple_of(m * tile, tile), tile)
            applied[here, :] += jnp.dot(
                env[here, pl.ds(pl.multiple_of(at * rows, rows), rows)],
                got[k, pl.ds(pl.multiple_of(at * rows, rows), rows), :],
                preferred_element_type=jnp.float32,
            )

    def act_on(k):
        first, second = mix[k, 0], mix[k, 1]

        @pl.loop(0, rows // 32)
        def _(t):
            halves = []
            for half in range(2):
                terms = []
                for w in range(chain):
                    there = pl.ds(pl.multiple_of(w * rows + t * 32 + half * 16, 16), 16)
                    for q in range(per):
                        terms.append(applied[there, q * cols:(q + 1) * cols])
                    applied[there, :] = jnp.zeros((16, WIDE), jnp.float32)
                halves.append(jnp.concatenate(terms, axis=0))
            hi, lo = split(jnp.concatenate(halves, axis=1))
            mixed = (
                jnp.dot(first, hi, preferred_element_type=jnp.float32)
                + jnp.dot(first, lo, preferred_element_type=jnp.float32)
                + jnp.dot(second, hi, preferred_element_type=jnp.float32)
            )
            for half in range(2):
                here = pl.ds(pl.multiple_of(t * 32 + half * 16, 16), 16)
                for p in range(phys):
                    acted[here, p * cols:(p + 1) * cols] += mixed[p * 16:(p + 1) * 16, half * cols:(half + 1) * cols]

    @pl.loop(0, steps * chips + 1)
    def _(t):
        k, d = t // chips, t % chips

        @pl.when((d == 0) & (k + AHEAD < steps))
        def _():
            own_copy(k + AHEAD).wait()
            own_sends(k + AHEAD, start)

        @pl.when((d > 0) & (k < steps))
        def _():
            passes(k, d, 0, True, start)
            passes(k, d, 1, True, start)

        @pl.when(t > 0)
        def _():
            kk, dd = (t - 1) // chips, (t - 1) % chips

            @pl.loop(0, 4)
            def _(j):
                side, lane = j // 2, j % 2
                src = z - dd + 2 * dd * side
                at = src * 2 + lane
                valid = (src >= 0) & (src < chips) & near(at, b) & ((dd > 0) | (side == 0))

                @pl.when(valid)
                def _():
                    @pl.when(lane != c)
                    def _():
                        move(kk, at, 2, mate).wait_recv()

                    multiply(kk, at)

            @pl.when(dd == chips - 1)
            def _():
                act_on(kk)

    total = jnp.zeros((cols, 2 * cols), jnp.float32)
    for p in range(phys):
        hi, lo = split(acted[:, p * cols:(p + 1) * cols])
        mine = got[p // per, pl.ds(pl.multiple_of(b * rows, rows), rows), (p % per) * cols:(p % per + 1) * cols]
        total += lax.dot_general(
            mine, jnp.concatenate([hi, lo], axis=1), (((0,), (0,)), ((), ())),
            preferred_element_type=jnp.float32,
        )
    total = total[:, :cols] + total[:, cols:]
    for j in range(n_blk):
        part[j] = total[j * piece:(j + 1) * piece]

    def rs_copy(src, dst, off):
        return pltpu.make_async_remote_copy(
            src_ref=part.at[dst], dst_ref=rs_buf.at[src],
            send_sem=rs_send.at[off], recv_sem=rs_recv.at[src],
            device_id=(s, dst), device_id_type=MESH,
        )

    for off in range(1, n_blk):
        rs_copy(b, lax.rem(b + off, n_blk), off).start()
    summed = part[b]
    for off in range(1, n_blk):
        peer = lax.rem(b + off, n_blk)
        rs_copy(peer, peer, off).wait_recv()
        summed += rs_buf[peer]
    xs_buf[s] = summed

    def xs_copy(src, dst, off):
        return pltpu.make_async_remote_copy(
            src_ref=xs_buf.at[src], dst_ref=xs_buf.at[src],
            send_sem=xs_send.at[off], recv_sem=xs_recv.at[src],
            device_id=(dst, b), device_id_type=MESH,
        )

    for off in range(1, n_sect):
        xs_copy(s, lax.rem(s + off, n_sect), off).start()
    for off in range(1, n_sect):
        peer = lax.rem(s + off, n_sect)
        xs_copy(peer, peer, off).wait_recv()

    def ag_copy(src, dst, off):
        return pltpu.make_async_remote_copy(
            src_ref=xs_buf, dst_ref=all_buf.at[src],
            send_sem=ag_send.at[off], recv_sem=ag_recv.at[src],
            device_id=(s, dst), device_id_type=MESH,
        )

    for off in range(1, n_blk):
        ag_copy(b, lax.rem(b + off, n_blk), off).start()
    all_buf[b] = xs_buf[...]
    for off in range(1, n_blk):
        peer = lax.rem(b + off, n_blk)
        ag_copy(peer, peer, off).wait_recv()

    incoming = edge[...]
    leaving = edge[...]
    for sect in range(n_sect):
        inter = jnp.concatenate([all_buf[j, sect] for j in range(n_blk)], axis=0)
        scale = jnp.sqrt(jnp.float32(cols)) / jnp.sqrt(jnp.sum(inter * inter, keepdims=True) + 1e-06)
        incoming = jnp.where(sect <= s, leaving, incoming)
        leaving = jnp.where(
            sect <= s,
            jnp.dot(leaving, inter * scale, precision=lax.Precision.HIGHEST, preferred_element_type=jnp.float32),
            leaving,
        )
    outgoing[0] = leaving

    hi, lo = split(incoming)
    weights = jnp.concatenate(
        [jnp.concatenate([hi, lo], axis=1), jnp.concatenate([hi, jnp.zeros_like(lo)], axis=1)], axis=0
    )
    for p in range(phys):
        hi, lo = split(acted[:, p * cols:(p + 1) * cols])
        res = jnp.dot(jnp.concatenate([hi, lo], axis=1), weights, preferred_element_type=jnp.float32)
        out[0, :, p * cols:(p + 1) * cols] = (res[:, :cols] + res[:, cols:]).astype(jnp.bfloat16)

    for off in range(1, n_blk):
        peer = lax.rem(b + off, n_blk)
        rs_copy(b, peer, off).wait_send()
        ag_copy(b, peer, off).wait_send()
    for off in range(1, n_sect):
        xs_copy(s, lax.rem(s + off, n_sect), off).wait_send()

    @pl.loop(0, steps)
    def _(k):
        own_sends(k, wait_sent)

        @pl.loop(1, chips)
        def _(d):
            passes(k, d, 0, False, wait_sent)
            passes(k, d, 1, False, wait_sent)


def per_device(n_sect, n_blk, theta, left_env, sector_ids, local_ops, edge_env):
    rows, width = theta.shape[1], theta.shape[2]
    chain, depth = left_env.shape[1], left_env.shape[3]
    phys = local_ops.shape[2]
    cols = width // phys
    steps = width // WIDE
    piece = cols // n_blk
    dims = (n_sect, n_blk, rows, depth, width, chain, phys, cols)
    my_sec = lax.dynamic_slice_in_dim(sector_ids[0], lax.axis_index("blk") * rows, rows, 0)[:, None]
    per = WIDE // cols
    flat = local_ops[0].reshape(chain, phys, steps, per).transpose(2, 1, 0, 3)
    hi = lax.reduce_precision(flat, 8, 7)
    pair = jnp.stack([hi, flat - hi], axis=1).astype(jnp.bfloat16)
    mix = pair[:, :, :, None, :, :, None] * jnp.eye(16, dtype=jnp.bfloat16)[:, None, None, :]
    mix = mix.reshape(steps, 2, phys * 16, chain * per * 16)
    any_spec = pl.BlockSpec(memory_space=pl.ANY)
    vmem = pl.BlockSpec(memory_space=pltpu.VMEM)
    dma = pltpu.SemaphoreType.DMA
    return pl.pallas_call(
        functools.partial(kernel, dims),
        out_shape=(
            jax.ShapeDtypeStruct((1, rows, width), jnp.bfloat16),
            jax.ShapeDtypeStruct((1, cols, cols), jnp.float32),
        ),
        in_specs=[any_spec, any_spec, vmem, vmem, vmem, vmem],
        out_specs=(vmem, vmem),
        scratch_shapes=[
            pltpu.VMEM((chain * rows, depth), jnp.bfloat16),
            pltpu.VMEM((steps, depth, WIDE), jnp.bfloat16),
            pltpu.VMEM((chain * rows, WIDE), jnp.float32),
            pltpu.VMEM((rows, width), jnp.float32),
            pltpu.VMEM((n_blk, piece, cols), jnp.float32),
            pltpu.VMEM((n_blk, piece, cols), jnp.float32),
            pltpu.VMEM((n_sect, piece, cols), jnp.float32),
            pltpu.VMEM((n_blk, n_sect, piece, cols), jnp.float32),
            dma((chain,)), dma((steps,)), dma((steps, n_blk)), dma((steps, n_blk, 3)),
            dma((n_blk,)), dma((n_blk,)), dma((n_sect,)), dma((n_sect,)), dma((n_blk,)), dma((n_blk,)),
        ],
        compiler_params=pltpu.CompilerParams(
            collective_id=0, has_side_effects=True, vmem_limit_bytes=63 * 1024 * 1024
        ),
        cost_estimate=pl.CostEstimate(
            flops=2 * chain * rows * depth * width,
            bytes_accessed=2 * chain * rows * depth,
            transcendentals=0,
        ),
    )(theta, left_env, my_sec, sector_ids, mix, edge_env)


def solution(mesh):
    placed = (
        P("sect", "blk", None),
        P("sect", None, "blk", None),
        P("sect", None),
        P("sect", None, None, None),
        P(),
    )
    return jax.shard_map(
        functools.partial(per_device, mesh.shape["sect"], mesh.shape["blk"]),
        mesh=mesh,
        in_specs=placed,
        out_specs=(P("sect", "blk", None), P("sect", None, None)),
        check_vma=False,
    )
```
